512 devices in a mesh: tens: 8 (over y, core), atom: 64 (over z, x).
Axes of the slice: x: 4, y: 4, z: 16, core: 2. Of those that a mesh axis runs over, the one named last changes fastest.
Arguments:
- chibar: float32 [384, 16384], P(None, 'atom'), may hold values from -6 to 6
- t_blocks: float32 [384, 786432], P(None, ('tens', 'atom')), may hold values from -0.3125 to 0.3125
- n_saved: float32 [384, 786432], P('tens', 'atom'), may hold values from -0.0390625 to 0.0390625
- q_list: int32 [8, 64, 3], P('tens', 'atom'), may hold values from 0 to 13, as said below
- q_count: int32 [8, 64], P('tens', 'atom'), may hold values from 1 to 3, as said below
Outputs:
- gbar: float32 [4096, 320], P('atom')
The draws below stay inside these ranges and needn't reach their ends.
Inputs may be any that keep to these rules, and one draw needn't show every extreme that they name: `q_list`: the 3 entries of one pair owner's list name blocks of 3 distinct atom indices. `q_count`: equal to 3 on at least one pair owner.
All inputs are finite; a program needn't handle non-finite values.
Results may differ from the reference program's by a relative error of at most 0.0003.
Values sent between devices are 32-bit elements; how exact they have to be, the bound alone decides.
A program may use at most 64 MiB of HBM per device.

```python
import jax
import jax.numpy as jnp
from jax import lax

BLK = 128
ORB_DEV = 64
QB_DEV = 2
REACH = 3
QL = 3
P_WIN = 384
NAUX = 16384
NORB = 4096
NU_T = 24
PAIR_DEV = 1536
N_TENS = 8
N_ATOM = 64
DEVICES = 512


def draw_q_list(key, part):
    owners = N_TENS * N_ATOM
    keys = jax.random.split(jax.random.fold_in(key, 11), owners)
    atoms = jax.vmap(lambda single: jax.random.permutation(single, 2 * REACH + 1)[:QL])(keys)
    within = jax.random.randint(jax.random.fold_in(key, 12), (owners, QL), 0, QB_DEV)
    slots = atoms * QB_DEV + within
    return slots.reshape(N_TENS, N_ATOM, QL).astype(jnp.int32)


def draw_q_count(key, part):
    owners = N_TENS * N_ATOM
    counts = jax.random.randint(jax.random.fold_in(key, 21), (owners,), 1, QL + 1)
    chosen_owner = jax.random.randint(jax.random.fold_in(key, 22), (), 0, owners)
    counts = jnp.where(jnp.arange(owners) == chosen_owner, QL, counts)
    return counts.reshape(N_TENS, N_ATOM).astype(jnp.int32)


def level_of(stream_key, extent, cuts, least, high):
    factor_of = 1.0
    for position, shards_of in cuts:
        draws = jax.random.uniform(jax.random.fold_in(jax.random.fold_in(stream_key, 6), position), (shards_of,), jnp.float32, least / len(cuts), high / len(cuts))
        factor_of = factor_of * jnp.repeat(jnp.exp(draws), extent[position] // shards_of).reshape((-1,) + (1,) * (len(extent) - 1 - position))
    return factor_of


def normal_values(stream_key, dims, deviation, reach, cuts=(), held_as=jnp.bfloat16):
    entries = deviation * jax.random.normal(stream_key, dims, jnp.float32)
    if cuts:
        entries = entries * level_of(stream_key, dims, cuts, -0.22, 0.18)
    return jnp.clip(entries, -reach, reach).astype(held_as)


def setup_inputs(seed: int = 0) -> dict:
    streams_of = jax.random.split(jax.random.key(seed), 6)
    chibar = normal_values(streams_of[0], (P_WIN, NAUX), 1.0, 6.0, ((1, 64),), jnp.float32)
    t_blocks = normal_values(streams_of[1], (QL * BLK, DEVICES * PAIR_DEV), (QL * BLK) ** -0.5, 0.3125, ((1, 512),), jnp.float32)
    n_saved = normal_values(streams_of[2], (P_WIN, NORB * 3 * ORB_DEV), (P_WIN * ORB_DEV) ** -0.5, 0.0390625, ((0, 8), (1, 64)), jnp.float32)
    q_list = draw_q_list(jax.random.fold_in(streams_of[5], 71), 0)
    q_count = draw_q_count(jax.random.fold_in(streams_of[5], 71), 0)
    return {"chibar": chibar, "t_blocks": t_blocks, "n_saved": n_saved, "q_list": q_list, "q_count": q_count}


def place_block(block, offset, orb_width):
    return jnp.pad(block, ((0, 0), (0, 0), (offset * orb_width, (2 - offset) * orb_width)))


def reference(chibar, t_blocks, n_saved, q_list, q_count):
    highest = lax.Precision.HIGHEST
    band_width = 3 * ORB_DEV
    column_blocks = chibar.reshape(P_WIN, N_ATOM, QB_DEV * BLK)
    tensor_view = t_blocks.reshape(QL * BLK, N_TENS, N_ATOM, PAIR_DEV)
    saved_view = n_saved.reshape(P_WIN, N_ATOM, ORB_DEV, band_width)
    offsets = jnp.arange(-REACH, REACH + 1).astype(jnp.int32)

    def per_atom(atom_index):
        nearby = (atom_index + offsets) % N_ATOM
        neighbour = jnp.take(column_blocks, nearby.astype(jnp.int32), axis=1)
        neighbour = neighbour.reshape(P_WIN, (2 * REACH + 1) * QB_DEV, BLK)
        slot_ids = jnp.take(q_list, atom_index, axis=1)
        in_use = jnp.take(q_count, atom_index, axis=1)
        chosen = jnp.take(neighbour, slot_ids.astype(jnp.int32), axis=1)
        keeper = (jnp.arange(QL)[None, :] < in_use[:, None]).astype(jnp.float32)
        chosen = (chosen * keeper[None, :, :, None]).reshape(P_WIN, N_TENS, QL * BLK)
        tensor_part = jnp.take(tensor_view, atom_index, axis=2)
        mbar = jnp.einsum("ptk,ktc->tpc", chosen, tensor_part, precision=highest)
        mbar = mbar.reshape(N_TENS, P_WIN, NU_T, ORB_DEV)
        saved_part = jnp.take(saved_view, atom_index, axis=1)
        partial_value = jnp.einsum("tpjm,pml->tjl", mbar, saved_part, precision=highest)
        return partial_value.reshape(band_width, band_width)

    partials = lax.map(per_atom, jnp.arange(N_ATOM).astype(jnp.int32))
    blocks = partials.reshape(N_ATOM, 3, ORB_DEV, band_width)
    from_lower = jnp.roll(blocks[:, 2], 1, axis=0)
    from_upper = jnp.roll(blocks[:, 0], -1, axis=0)
    result = place_block(from_lower, 0, ORB_DEV) + place_block(blocks[:, 1], 1, ORB_DEV) + place_block(from_upper, 2, ORB_DEV)
    return result.reshape(NORB, 5 * ORB_DEV)
```

```python
import jax
import jax.numpy as jnp
from jax import lax
from jax.experimental import pallas as pl
from jax.experimental.pallas import tpu as pltpu
from jax.sharding import PartitionSpec as P

F32 = jnp.float32
BF16 = jnp.bfloat16
MESH = pl.DeviceIdType.MESH
REACH = 3
STAGES = 4
SHIFTS = (1, -1, 2, -2, 3, -3)


def split(x):
    high = x.astype(BF16)
    return high, (x - high.astype(F32)).astype(BF16)


def dot(a, b):
    return jnp.dot(a, b, preferred_element_type=F32)


def dot3(a_high, a_low, b_high, b_low):
    return dot(a_high, b_high) + (dot(a_high, b_low) + dot(a_low, b_high))


def kernel(n_tens, n_atom, chibar, t_blocks, n_saved, q_list_in, q_count_in, out, q_list, q_count,
           t_full, t_high, t_low, n_full, n_left, n_right, n_high, n_low,
           near0, near1, near2, near3, past0, past1, past2, past3, mbar_out, mbar_in, part_out, part_in, home_in, total, final,
           q_sem, t_sem, n_sem, own_sem, chi_send, chi_recv, fwd_send, fwd_recv,
           mbar_send, mbar_recv, part_send, part_recv, home_send, home_recv, fin_send, fin_recv):
    near = (near0, near1, near2, near3)
    past = (past0, past1, past2, past3)
    t = lax.axis_index("tens")
    s = lax.axis_index("atom")
    y = t // 2
    c = lax.rem(t, 2)
    chips = n_tens // 2

    def device(chip, core):
        return lax.rem(chip + chips, chips) * 2 + core

    def atom(by):
        return lax.rem(s + by + n_atom, n_atom)

    chip_to = (y + 2, y + 1 - 2 * c, y - 1 + 2 * c, y)
    chip_to2 = (y + 2, y - 1 + 2 * c, y + 1 - 2 * c, y)
    chip_from = (y + 2, y - 1 + 2 * c, y + 1 - 2 * c, y)

    def target(k, e):
        return device(chip_to[k], c) if e == 0 else device(chip_to2[k], 1 - c)

    def source(k, e):
        return device(chip_from[k], c if e == 0 else 1 - c)

    sibling = device(y, 1 - c)

    load_q = (pltpu.make_async_copy(q_list_in, q_list, q_sem.at[0]), pltpu.make_async_copy(q_count_in, q_count, q_sem.at[1]))
    for copy in load_q:
        copy.start()
    load_t = pltpu.make_async_copy(t_blocks, t_full, t_sem)
    load_n = pltpu.make_async_copy(n_saved, n_full, n_sem)
    load_t.start()
    own = []
    for k in range(STAGES):
        rows = pl.ds(pl.multiple_of(target(k, 0) * 48, 48), 48)
        own.append(pltpu.make_async_copy(chibar.at[rows], near[k].at[REACH], own_sem.at[k]))
        own[k].start()
    load_n.start()

    barrier = pltpu.get_barrier_semaphore()
    for by in SHIFTS:
        pl.semaphore_signal(barrier, inc=1, device_id=(t, atom(by)), device_id_type=MESH)
    for by in range(1, n_tens):
        pl.semaphore_signal(barrier, inc=1, device_id=(lax.rem(t + by, n_tens), s), device_id_type=MESH)
    pl.semaphore_wait(barrier, len(SHIFTS) + n_tens - 1)

    chi = []
    for k in range(STAGES):
        rows = pl.ds(pl.multiple_of(target(k, 0) * 48, 48), 48)
        chi.append([
            pltpu.make_async_remote_copy(
                src_ref=chibar.at[rows],
                dst_ref=near[k].at[REACH - by],
                send_sem=chi_send.at[k, i],
                recv_sem=chi_recv.at[k, i],
                device_id=(t, atom(by)),
                device_id_type=MESH,
            )
            for i, by in enumerate(SHIFTS)
        ])
    for copy in chi[0]:
        copy.start()

    load_t.wait()

    def split_t(i, _):
        rows = pl.ds(pl.multiple_of(i * 16, 16), 16)
        t_high[rows], t_low[rows] = split(t_full[rows])
        return _

    lax.fori_loop(0, 24, split_t, 0)
    low_half = lax.broadcasted_iota(jnp.int32, (8, 128), 1) < 64

    def lay_n(m, _):
        base = pl.multiple_of(m * 384, 384)
        for p in range(6):
            rows = pl.ds(p * 8, 8)
            first = n_full[rows, pl.ds(base, 128)]
            second = n_full[rows, pl.ds(base + 128, 128)]
            third = n_full[rows, pl.ds(base + 256, 128)]
            second_r = pltpu.roll(second, 64, 1)
            third_r = pltpu.roll(third, 64, 1)
            start = (p % 3) * 8 * 128 + (p // 3) * 64 + 2 * m
            n_left[pl.ds(start, 8, stride=128), :] = first
            n_right[pl.ds(start, 8, stride=128), :] = second
            n_left[pl.ds(start + 1, 8, stride=128), :] = jnp.where(low_half, second_r, third_r)
            n_right[pl.ds(start + 1, 8, stride=128), :] = third_r
        return _

    def split_n(i, _):
        rows = pl.ds(pl.multiple_of(i * 64, 64), 64)
        n_high[rows, 0:128], n_low[rows, 0:128] = split(n_left[rows])
        n_high[rows, 128:256], n_low[rows, 128:256] = split(n_right[rows])
        return _


    mbar = []
    for k in range(STAGES):
        mbar.append([
            pltpu.make_async_remote_copy(
                src_ref=mbar_out.at[2 * k + e],
                dst_ref=mbar_in.at[2 * k + e],
                send_sem=mbar_send.at[2 * k + e],
                recv_sem=mbar_recv.at[2 * k + e],
                device_id=(target(k, e), s),
                device_id_type=MESH,
            )
            for e in range(2)
        ])

    forward = [
        pltpu.make_async_remote_copy(
            src_ref=near[k],
            dst_ref=past[k],
            send_sem=fwd_send.at[k],
            recv_sem=fwd_recv.at[k],
            device_id=(sibling, s),
            device_id_type=MESH,
        )
        for k in range(STAGES)
    ]
    half_of = lax.broadcasted_iota(jnp.int32, (24, 128), 1) < 64

    def compute(k, e):
        pieces = []
        for q in range(3):
            name = q_list[0, 0, q]
            block = (past if e else near)[k][name // 2]
            piece = jnp.where(lax.rem(name, 2) == 0, block[:, :128], block[:, 128:])
            pieces.append(jnp.where(q < q_count[0, 0], piece, jnp.zeros_like(piece)))
        high, low = split(jnp.concatenate(pieces, axis=1))
        for j in range(6):
            cols = pl.ds(j * 256, 256)
            r = dot3(high, low, t_high[:, cols], t_low[:, cols])
            for i in range(2):
                r0 = r[:24, i * 128:(i + 1) * 128]
                r1 = r[24:, i * 128:(i + 1) * 128]
                even = jnp.where(half_of, r0, pltpu.roll(r1, 64, 1))
                odd = jnp.where(half_of, pltpu.roll(r0, 64, 1), r1)
                nu = j * 4 + i * 2
                for g in range(3):
                    mbar_out[2 * k + e, pl.ds(g * 192 + nu, 8, stride=24), :] = even[g * 8:(g + 1) * 8]
                    mbar_out[2 * k + e, pl.ds(g * 192 + nu + 1, 8, stride=24), :] = odd[g * 8:(g + 1) * 8]

    for copy in load_q:
        copy.wait()
    for k in range(STAGES):
        own[k].wait()
        for copy in chi[k]:
            copy.wait_recv()
        forward[k].start()
        if k < 3:
            for copy in chi[k + 1]:
                copy.start()
        compute(k, 0)
        if k < 3:
            mbar[k][0].start()
        forward[k].wait_recv()
        compute(k, 1)
        mbar[k][1].start()
        if k == 0:
            load_n.wait()
            lax.fori_loop(0, 32, lay_n, 0)
        if k == 1:
            lax.fori_loop(0, 48, split_n, 0)

    def side(o):
        return jnp.where(o < 3, -1, jnp.where(o > 4, 1, 0))

    def straddles(o):
        return jnp.logical_or(o == 2, o == 5)

    def part(i, o):
        return pltpu.make_async_remote_copy(
            src_ref=part_out.at[i], dst_ref=part_in.at[i], send_sem=part_send.at[i], recv_sem=part_recv.at[i],
            device_id=(o, atom(side(o))), device_id_type=MESH)

    def part_home(i, o):
        return pltpu.make_async_remote_copy(
            src_ref=part_out.at[i], dst_ref=home_in.at[i], send_sem=home_send.at[i], recv_sem=home_recv.at[i],
            device_id=(o, s), device_id_type=MESH)

    inner = side(t) == 0
    edge = straddles(t)

    for k in (0, 3, 1, 2):
        if k < 3:
            mbar[k][0].wait_recv()
        mbar[k][1].wait_recv()
        first = mbar_out if k == 3 else mbar_in
        acc = jnp.zeros((48, 256), F32)
        for g in range(6):
            highs, lows = [], []
            for p in range(4):
                rows = pl.ds((g * 4 + p) * 24, 24)
                high, low = split(jnp.concatenate([first[2 * k, rows, :], mbar_in[2 * k + 1, rows, :]], axis=0))
                highs.append(high)
                lows.append(low)
            rows = pl.ds(g * 512, 512)
            acc = acc + dot3(jnp.concatenate(highs, axis=1), jnp.concatenate(lows, axis=1), n_high[rows], n_low[rows])
        part_out[2 * k] = acc[:24]
        part_out[2 * k + 1] = acc[24:]
        for e in range(2):
            i, o = 2 * k + e, source(k, e)
            if i == 6:
                @pl.when(jnp.logical_not(inner))
                def _():
                    part(6, t).start()
            else:
                part(i, o).start()

                @pl.when(straddles(o))
                def _():
                    part_home(i, o).start()

    order = (0, 1, 7, 2, 3, 4, 5)

    @pl.when(inner)
    def _():
        part_in[6] = part_out[6]

    @pl.when(jnp.logical_not(inner))
    def _():
        part(6, t).wait_recv()

    summed = part_in[6]
    for i in order:
        part(i, source(i // 2, i % 2)).wait_recv()
        summed = summed + part_in[i]
    total[...] = summed

    @pl.when(edge)
    def _():
        near_sum = part_out[6]
        for i in order:
            part_home(i, source(i // 2, i % 2)).wait_recv()
            near_sum = near_sum + home_in[i]
        row = lax.broadcasted_iota(jnp.int32, (24, 256), 0)
        least = jnp.where(t == 2, 16, 0)
        from_home = jnp.logical_and(row >= least, row < least + 8)
        total[...] = jnp.where(from_home, near_sum, total[...])

    def share(i):
        return pltpu.make_async_remote_copy(
            src_ref=total, dst_ref=final.at[t], send_sem=fin_send.at[i], recv_sem=fin_recv.at[n_tens - i],
            device_id=(lax.rem(t + i, n_tens), s), device_id_type=MESH)

    for i in (4, 3, 5, 2, 6, 1, 7):
        share(i).start()
    final[t] = total[...]
    for i in range(1, n_tens):
        share(i).wait_recv()

    lower = jnp.concatenate([final[5, 8:24, :], final[6], final[7]], axis=0)
    mid = jnp.concatenate([final[2, 16:24, :], final[3], final[4], final[5, 0:8, :]], axis=0)
    upper = jnp.concatenate([final[0], final[1], final[2, 0:16, :]], axis=0)
    half = lax.broadcasted_iota(jnp.int32, (64, 128), 1) < 64
    mid0 = pltpu.roll(mid[:, :128], 64, 1)
    mid1 = pltpu.roll(mid[:, 128:], 64, 1)
    zero = jnp.zeros((64, 128), F32)
    out[:, 0:128] = lower[:, :128] + jnp.where(half, zero, mid0)
    out[:, 128:256] = jnp.where(half, lower[:, 128:], zero) + jnp.where(half, mid0, mid1) + upper[:, :128]
    out[:, 256:320] = upper[:, 128:192]

    for k in range(STAGES):
        for copy in chi[k]:
            copy.wait_send()
        forward[k].wait_send()
        for e in range(2):
            if (k, e) != (3, 0):
                mbar[k][e].wait_send()
    for i in order:
        o = source(i // 2, i % 2)
        part(i, o).wait_send()

        @pl.when(straddles(o))
        def _():
            part_home(i, o).wait_send()

    @pl.when(jnp.logical_not(inner))
    def _():
        part(6, t).wait_send()

    for i in range(1, n_tens):
        share(i).wait_send()


def local(n_tens, n_atom, chibar, t_blocks, n_saved, q_list, q_count):
    def body(*refs):
        kernel(n_tens, n_atom, *refs)

    hbm = pl.BlockSpec(memory_space=pltpu.HBM)
    dma = pltpu.SemaphoreType.DMA
    return pl.pallas_call(
        body,
        out_shape=jax.ShapeDtypeStruct((64, 320), F32),
        in_specs=[hbm] * 5,
        out_specs=pl.BlockSpec(memory_space=pltpu.VMEM),
        scratch_shapes=[
            pltpu.SMEM((1, 1, 3), jnp.int32),
            pltpu.SMEM((1, 1), jnp.int32),
            pltpu.VMEM((384, 1536), F32),
            pltpu.VMEM((384, 1536), BF16),
            pltpu.VMEM((384, 1536), BF16),
            pltpu.VMEM((48, 12288), F32),
            pltpu.VMEM((3072, 128), F32),
            pltpu.VMEM((3072, 128), F32),
            pltpu.VMEM((3072, 256), BF16),
            pltpu.VMEM((3072, 256), BF16),
        ]
        + [pltpu.VMEM((7, 48, 256), F32)] * (2 * STAGES)
        + [
            pltpu.VMEM((8, 576, 128), F32),
            pltpu.VMEM((8, 576, 128), F32),
            pltpu.VMEM((8, 24, 256), F32),
            pltpu.VMEM((8, 24, 256), F32),
            pltpu.VMEM((8, 24, 256), F32),
            pltpu.VMEM((24, 256), F32),
            pltpu.VMEM((8, 24, 256), F32),
            dma((2,)), dma, dma, dma((STAGES,)), dma((STAGES, 6)), dma((STAGES, 6)), dma((STAGES,)), dma((STAGES,)),
            dma((8,)), dma((8,)), dma((8,)), dma((8,)), dma((8,)), dma((8,)), dma((8,)), dma((8,)),
        ],
        compiler_params=pltpu.CompilerParams(
            collective_id=0, has_side_effects=True, vmem_limit_bytes=63 * 2**20
        ),
        name="gradient",
    )(chibar, t_blocks, n_saved, q_list, q_count)


def solution(mesh):
    sizes = mesh.shape
    placed = (
        P(None, "atom"),
        P(None, ("tens", "atom")),
        P("tens", "atom"),
        P("tens", "atom", None),
        P("tens", "atom"),
    )

    def step(*args):
        return local(sizes["tens"], sizes["atom"], *args)

    return jax.shard_map(step, mesh=mesh, in_specs=placed, out_specs=P("atom", None), check_vma=False)
```

```python
import jax
import jax.numpy as jnp
from jax import lax
from jax.experimental import pallas as pl
from jax.experimental.pallas import tpu as pltpu
from jax.sharding import PartitionSpec as P

F32 = jnp.float32
BF16 = jnp.bfloat16
MESH = pl.DeviceIdType.MESH
REACH = 3
STAGES = 4
STEPS = ((0, 0, 16), (0, 16, 32), (1, 0, 48), (2, 0, 48), (3, 0, 48))
SHIFTS = (1, -1, 2, -2, 3, -3)


def split(x):
    high = x.astype(BF16)
    return high, (x - high.astype(F32)).astype(BF16)


def dot(a, b):
    return jnp.dot(a, b, preferred_element_type=F32)


def dot3(a_high, a_low, b_high, b_low):
    rows = a_high.shape[0]
    both = dot(jnp.concatenate([a_high, a_low], axis=0), b_high)
    return both[:rows] + (both[rows:] + dot(a_high, b_low))


def kernel(n_tens, n_atom, chibar, t_blocks, n_saved, q_list_in, q_count_in, out, q_list, q_count,
           t_full, t_high, t_low, n_full, n_left, n_right, n_high, n_low,
           near0, near1, near2, near3, near4, past0, past1, past2, past3, past4, mbar_out, mbar_in, part_out, part_in, home_in, total, final,
           q_sem, t_sem, n_sem, own_sem, chi_send, chi_recv, fwd_send, fwd_recv,
           mbar_send, mbar_recv, part_send, part_recv, home_send, home_recv, fin_send, fin_recv):
    near = (near0, near1, near2, near3, near4)
    past = (past0, past1, past2, past3, past4)
    t = lax.axis_index("tens")
    s = lax.axis_index("atom")
    y = t // 2
    c = lax.rem(t, 2)
    chips = n_tens // 2

    def device(chip, core):
        return lax.rem(chip + chips, chips) * 2 + core

    def atom(by):
        return lax.rem(s + by + n_atom, n_atom)

    chip_to = (y + 2, y + 1 - 2 * c, y - 1 + 2 * c, y)
    chip_to2 = (y + 2, y - 1 + 2 * c, y + 1 - 2 * c, y)
    chip_from = (y + 2, y - 1 + 2 * c, y + 1 - 2 * c, y)

    def target(k, e):
        return device(chip_to[k], c) if e == 0 else device(chip_to2[k], 1 - c)

    def source(k, e):
        return device(chip_from[k], c if e == 0 else 1 - c)

    sibling = device(y, 1 - c)

    load_q = (pltpu.make_async_copy(q_list_in, q_list, q_sem.at[0]), pltpu.make_async_copy(q_count_in, q_count, q_sem.at[1]))
    load_t = pltpu.make_async_copy(t_blocks, t_full, t_sem)
    load_n = pltpu.make_async_copy(n_saved, n_full, n_sem)
    own = []

    def rows_of(step):
        k, first, rows = STEPS[step]
        return pl.ds(pl.multiple_of(target(k, 0) * 48 + first, 16), rows)

    for i in range(len(STEPS)):
        own.append(pltpu.make_async_copy(chibar.at[rows_of(i)], near[i].at[REACH], own_sem.at[i]))
        own[i].start()
    load_t.start()
    load_n.start()
    for copy in load_q:
        copy.start()

    low_half = lax.broadcasted_iota(jnp.int32, (8, 128), 1) < 64

    def prepare():
        load_t.wait()

        def split_t(i, _):
            rows = pl.ds(pl.multiple_of(i * 16, 16), 16)
            t_high[rows], t_low[rows] = split(t_full[rows])
            return _

        lax.fori_loop(0, 24, split_t, 0)


    def lay_n(m, _):
        base = pl.multiple_of(m * 384, 384)
        for p in range(6):
            rows = pl.ds(p * 8, 8)
            first = n_full[rows, pl.ds(base, 128)]
            second = n_full[rows, pl.ds(base + 128, 128)]
            third = n_full[rows, pl.ds(base + 256, 128)]
            second_r = pltpu.roll(second, 64, 1)
            third_r = pltpu.roll(third, 64, 1)
            start = (p // 2) * 8 * 128 + (p % 2) * 64 + 2 * m
            n_left[pl.ds(start, 8, stride=128), :] = first
            n_right[pl.ds(start, 8, stride=128), :] = second
            n_left[pl.ds(start + 1, 8, stride=128), :] = jnp.where(low_half, second_r, third_r)
            n_right[pl.ds(start + 1, 8, stride=128), :] = third_r
        return _


    def split_n(i, _):
        rows = pl.ds(pl.multiple_of(i * 64, 64), 64)
        n_high[rows, 0:128], n_low[rows, 0:128] = split(n_left[rows])
        n_high[rows, 128:256], n_low[rows, 128:256] = split(n_right[rows])
        return _

    barrier = pltpu.get_barrier_semaphore()
    for by in SHIFTS:
        pl.semaphore_signal(barrier, inc=1, device_id=(t, atom(by)), device_id_type=MESH)
    for by in range(1, n_tens):
        pl.semaphore_signal(barrier, inc=1, device_id=(lax.rem(t + by, n_tens), s), device_id_type=MESH)
    pl.semaphore_wait(barrier, len(SHIFTS) + n_tens - 1)

    chi = [
        [
            pltpu.make_async_remote_copy(
                src_ref=near[step].at[REACH],
                dst_ref=near[step].at[REACH - by],
                send_sem=chi_send.at[step, i],
                recv_sem=chi_recv.at[step, i],
                device_id=(t, atom(by)),
                device_id_type=MESH,
            )
            for i, by in enumerate(SHIFTS)
        ]
        for step in range(len(STEPS))
    ]
    for copy in own:
        copy.wait()
    for step in (0, 1):
        for copy in chi[step]:
            copy.start()
    prepare()

    def mbar(step, e):
        k, first, rows = STEPS[step]
        part_rows = pl.ds(first * 12, rows * 12)
        return pltpu.make_async_remote_copy(
            src_ref=mbar_out.at[2 * k + e, part_rows],
            dst_ref=mbar_in.at[2 * k + e, part_rows],
            send_sem=mbar_send.at[2 * step + e],
            recv_sem=mbar_recv.at[2 * step + e],
            device_id=(target(k, e), s),
            device_id_type=MESH,
        )

    forward = [
        pltpu.make_async_remote_copy(
            src_ref=near[i],
            dst_ref=past[i],
            send_sem=fwd_send.at[i],
            recv_sem=fwd_recv.at[i],
            device_id=(sibling, s),
            device_id_type=MESH,
        )
        for i in range(len(STEPS))
    ]

    def compute(step, e):
        k, first, rows = STEPS[step]
        pieces = []
        for q in range(3):
            name = q_list[0, 0, q]
            block = (past if e else near)[step][name // 2]
            piece = jnp.where(lax.rem(name, 2) == 0, block[:, :128], block[:, 128:])
            pieces.append(jnp.where(q < q_count[0, 0], piece, jnp.zeros_like(piece)))
        high, low = split(jnp.concatenate(pieces, axis=1))
        for j in range(6):
            cols = pl.ds(j * 256, 256)
            r = dot3(high, low, t_high[:, cols], t_low[:, cols])
            for g in range(rows // 16):
                for i in range(2):
                    r0 = r[g * 16:g * 16 + 8, i * 128:(i + 1) * 128]
                    r1 = r[g * 16 + 8:g * 16 + 16, i * 128:(i + 1) * 128]
                    even = jnp.where(low_half, r0, pltpu.roll(r1, 64, 1))
                    odd = jnp.where(low_half, pltpu.roll(r0, 64, 1), r1)
                    at = first * 12 + g * 192 + j * 4 + i * 2
                    mbar_out[2 * k + e, pl.ds(at, 8, stride=24), :] = even
                    mbar_out[2 * k + e, pl.ds(at + 1, 8, stride=24), :] = odd

    steps_of = ((0, 1), (2,), (3,), (4,))

    def side(o):
        return jnp.where(o < 3, -1, jnp.where(o > 4, 1, 0))

    def straddles(o):
        return jnp.logical_or(o == 2, o == 5)

    def part(i, o):
        return pltpu.make_async_remote_copy(
            src_ref=part_out.at[i], dst_ref=part_in.at[i], send_sem=part_send.at[i], recv_sem=part_recv.at[i],
            device_id=(o, atom(side(o))), device_id_type=MESH)

    def part_home(i, o):
        return pltpu.make_async_remote_copy(
            src_ref=part_out.at[i], dst_ref=home_in.at[i], send_sem=home_send.at[i], recv_sem=home_recv.at[i],
            device_id=(o, s), device_id_type=MESH)

    inner = side(t) == 0
    edge = straddles(t)

    def contract(k):
        for step in steps_of[k]:
            if k < 3:
                mbar(step, 0).wait_recv()
            mbar(step, 1).wait_recv()
        first = mbar_out if k == 3 else mbar_in
        acc = jnp.zeros((48, 256), F32)
        for g in range(6):
            highs, lows = [], []
            for p in range(4):
                rows = pl.ds((g * 4 + p) * 24, 24)
                high, low = split(jnp.concatenate([first[2 * k, rows, :], mbar_in[2 * k + 1, rows, :]], axis=0))
                highs.append(high)
                lows.append(low)
            rows = pl.ds(g * 512, 512)
            acc = acc + dot3(jnp.concatenate(highs, axis=1), jnp.concatenate(lows, axis=1), n_high[rows], n_low[rows])
        part_out[2 * k] = acc[:24]
        part_out[2 * k + 1] = acc[24:]
        for e in range(2):
            i, o = 2 * k + e, source(k, e)
            if i == 6:
                @pl.when(jnp.logical_not(inner))
                def _():
                    part(6, t).start()
            else:
                part(i, o).start()

                @pl.when(straddles(o))
                def _():
                    part_home(i, o).start()

    def settle():
        for step in range(len(STEPS)):
            for copy in chi[step]:
                copy.wait_send()
            forward[step].wait_send()

    def fetch(step):
        for copy in chi[step]:
            copy.start()

    for copy in load_q:
        copy.wait()
    for step in range(len(STEPS)):
        for copy in chi[step]:
            copy.wait_recv()
        forward[step].start()
        for later in ((2,), (3,), (4,), (), ())[step]:
            fetch(later)
        compute(step, 0)
        if step < 4:
            mbar(step, 0).start()
        forward[step].wait_recv()
        compute(step, 1)
        mbar(step, 1).start()
        if step == 0:
            load_n.wait()
        if step < 4:
            lax.fori_loop(8 * step, 8 * step + 8, lay_n, 0)
        else:
            lax.fori_loop(0, 48, split_n, 0)

    settle()
    for k in (3, 0, 1, 2):
        contract(k)

    for step in range(len(STEPS)):
        if step < 4:
            mbar(step, 0).wait_send()
        mbar(step, 1).wait_send()

    order = (0, 1, 7, 2, 3, 4, 5)

    @pl.when(inner)
    def _():
        part_in[6] = part_out[6]

    @pl.when(jnp.logical_not(inner))
    def _():
        part(6, t).wait_recv()

    summed = part_in[6]
    for i in order:
        part(i, source(i // 2, i % 2)).wait_recv()
        summed = summed + part_in[i]
    total[...] = summed

    @pl.when(edge)
    def _():
        near_sum = part_out[6]
        for i in order:
            part_home(i, source(i // 2, i % 2)).wait_recv()
            near_sum = near_sum + home_in[i]
        row = lax.broadcasted_iota(jnp.int32, (24, 256), 0)
        least = jnp.where(t == 2, 16, 0)
        from_home = jnp.logical_and(row >= least, row < least + 8)
        total[...] = jnp.where(from_home, near_sum, total[...])

    def share(i):
        return pltpu.make_async_remote_copy(
            src_ref=total, dst_ref=final.at[t], send_sem=fin_send.at[i], recv_sem=fin_recv.at[n_tens - i],
            device_id=(lax.rem(t + i, n_tens), s), device_id_type=MESH)

    for i in (4, 3, 5, 2, 6, 1, 7):
        share(i).start()
    final[t] = total[...]
    for i in order:
        o = source(i // 2, i % 2)
        part(i, o).wait_send()

        @pl.when(straddles(o))
        def _():
            part_home(i, o).wait_send()

    @pl.when(jnp.logical_not(inner))
    def _():
        part(6, t).wait_send()

    for i in range(1, n_tens):
        share(i).wait_recv()

    lower = jnp.concatenate([final[5, 8:24, :], final[6], final[7]], axis=0)
    mid = jnp.concatenate([final[2, 16:24, :], final[3], final[4], final[5, 0:8, :]], axis=0)
    upper = jnp.concatenate([final[0], final[1], final[2, 0:16, :]], axis=0)
    half = lax.broadcasted_iota(jnp.int32, (64, 128), 1) < 64
    mid0 = pltpu.roll(mid[:, :128], 64, 1)
    mid1 = pltpu.roll(mid[:, 128:], 64, 1)
    zero = jnp.zeros((64, 128), F32)
    out[:, 0:128] = lower[:, :128] + jnp.where(half, zero, mid0)
    out[:, 128:256] = jnp.where(half, lower[:, 128:], zero) + jnp.where(half, mid0, mid1) + upper[:, :128]
    out[:, 256:320] = upper[:, 128:192]

    for i in range(1, n_tens):
        share(i).wait_send()


def local(n_tens, n_atom, chibar, t_blocks, n_saved, q_list, q_count):
    def body(*refs):
        kernel(n_tens, n_atom, *refs)

    hbm = pl.BlockSpec(memory_space=pltpu.HBM)
    dma = pltpu.SemaphoreType.DMA
    return pl.pallas_call(
        body,
        out_shape=jax.ShapeDtypeStruct((64, 320), F32),
        in_specs=[hbm] * 5,
        out_specs=pl.BlockSpec(memory_space=pltpu.VMEM),
        scratch_shapes=[
            pltpu.SMEM((1, 1, 3), jnp.int32),
            pltpu.SMEM((1, 1), jnp.int32),
            pltpu.VMEM((384, 1536), F32),
            pltpu.VMEM((384, 1536), BF16),
            pltpu.VMEM((384, 1536), BF16),
            pltpu.VMEM((48, 12288), F32),
            pltpu.VMEM((3072, 128), F32),
            pltpu.VMEM((3072, 128), F32),
            pltpu.VMEM((3072, 256), BF16),
            pltpu.VMEM((3072, 256), BF16),
        ]
        + [pltpu.VMEM((7, rows, 256), F32) for _, _, rows in STEPS] * 2
        + [
            pltpu.VMEM((8, 576, 128), F32),
            pltpu.VMEM((8, 576, 128), F32),
            pltpu.VMEM((8, 24, 256), F32),
            pltpu.VMEM((8, 24, 256), F32),
            pltpu.VMEM((8, 24, 256), F32),
            pltpu.VMEM((24, 256), F32),
            pltpu.VMEM((8, 24, 256), F32),
            dma((2,)), dma, dma, dma((5,)), dma((5, 6)), dma((5, 6)), dma((5,)), dma((5,)),
            dma((10,)), dma((10,)), dma((8,)), dma((8,)), dma((8,)), dma((8,)), dma((8,)), dma((8,)),
        ],
        compiler_params=pltpu.CompilerParams(
            collective_id=0, has_side_effects=True, vmem_limit_bytes=63 * 2**20
        ),
        name="gradient",
    )(chibar, t_blocks, n_saved, q_list, q_count)


def solution(mesh):
    sizes = mesh.shape
    placed = (
        P(None, "atom"),
        P(None, ("tens", "atom")),
        P("tens", "atom"),
        P("tens", "atom", None),
        P("tens", "atom"),
    )

    def step(*args):
        return local(sizes["tens"], sizes["atom"], *args)

    return jax.shard_map(step, mesh=mesh, in_specs=placed, out_specs=P("atom", None), check_vma=False)
```

```python
import jax
import jax.numpy as jnp
from jax import lax
from jax.experimental import pallas as pl
from jax.experimental.pallas import tpu as pltpu
from jax.sharding import PartitionSpec as P

F32 = jnp.float32
BF16 = jnp.bfloat16
MESH = pl.DeviceIdType.MESH
REACH = 3
STAGES = 4
SHIFTS = (1, -1, 2, -2, 3, -3)


def split(x):
    high = x.astype(BF16)
    return high, (x - high.astype(F32)).astype(BF16)


def dot(a, b):
    return jnp.dot(a, b, preferred_element_type=F32)


def dot3(a_high, a_low, b_high, b_low):
    rows = a_high.shape[0]
    both = dot(jnp.concatenate([a_high, a_low], axis=0), b_high)
    return both[:rows] + (both[rows:] + dot(a_high, b_low))


def kernel(n_tens, n_atom, chibar, t_blocks, n_saved, q_list_in, q_count_in, out, q_list, q_count,
           t_full, t_high, t_low, n_full, n_left, n_right, n_high, n_low,
           near0, near1, near2, near3, past0, past1, past2, past3, mbar_out, mbar_in, part_out, part_in, home_in, total, final,
           q_sem, t_sem, n_sem, own_sem, chi_send, chi_recv, fwd_send, fwd_recv,
           mbar_send, mbar_recv, part_send, part_recv, home_send, home_recv, fin_send, fin_recv):
    near = (near0, near1, near2, near3)
    past = (past0, past1, past2, past3)
    t = lax.axis_index("tens")
    s = lax.axis_index("atom")
    y = t // 2
    c = lax.rem(t, 2)
    chips = n_tens // 2

    def device(chip, core):
        return lax.rem(chip + chips, chips) * 2 + core

    def atom(by):
        return lax.rem(s + by + n_atom, n_atom)

    chip_to = (y + 2, y + 1 - 2 * c, y - 1 + 2 * c, y)
    chip_to2 = (y + 2, y - 1 + 2 * c, y + 1 - 2 * c, y)
    chip_from = (y + 2, y - 1 + 2 * c, y + 1 - 2 * c, y)

    def target(k, e):
        return device(chip_to[k], c) if e == 0 else device(chip_to2[k], 1 - c)

    def source(k, e):
        return device(chip_from[k], c if e == 0 else 1 - c)

    sibling = device(y, 1 - c)

    load_q = (pltpu.make_async_copy(q_list_in, q_list, q_sem.at[0]), pltpu.make_async_copy(q_count_in, q_count, q_sem.at[1]))
    for copy in load_q:
        copy.start()
    load_t = pltpu.make_async_copy(t_blocks, t_full, t_sem)
    load_n = pltpu.make_async_copy(n_saved, n_full, n_sem)
    load_t.start()
    own = []
    for k in range(STAGES):
        rows = pl.ds(pl.multiple_of(target(k, 0) * 48, 48), 48)
        own.append(pltpu.make_async_copy(chibar.at[rows], near[k].at[REACH], own_sem.at[k]))
        own[k].start()
    load_n.start()

    barrier = pltpu.get_barrier_semaphore()
    for by in SHIFTS:
        pl.semaphore_signal(barrier, inc=1, device_id=(t, atom(by)), device_id_type=MESH)
    for by in range(1, n_tens):
        pl.semaphore_signal(barrier, inc=1, device_id=(lax.rem(t + by, n_tens), s), device_id_type=MESH)
    pl.semaphore_wait(barrier, len(SHIFTS) + n_tens - 1)

    chi = []
    for k in range(STAGES):
        rows = pl.ds(pl.multiple_of(target(k, 0) * 48, 48), 48)
        chi.append([
            pltpu.make_async_remote_copy(
                src_ref=chibar.at[rows],
                dst_ref=near[k].at[REACH - by],
                send_sem=chi_send.at[k, i],
                recv_sem=chi_recv.at[k, i],
                device_id=(t, atom(by)),
                device_id_type=MESH,
            )
            for i, by in enumerate(SHIFTS)
        ])
    for copy in chi[0]:
        copy.start()

    load_t.wait()

    def split_t(i, _):
        rows = pl.ds(pl.multiple_of(i * 16, 16), 16)
        t_high[rows], t_low[rows] = split(t_full[rows])
        return _

    lax.fori_loop(0, 24, split_t, 0)
    low_half = lax.broadcasted_iota(jnp.int32, (8, 128), 1) < 64

    def lay_n(m, _):
        base = pl.multiple_of(m * 384, 384)
        for p in range(6):
            rows = pl.ds(p * 8, 8)
            first = n_full[rows, pl.ds(base, 128)]
            second = n_full[rows, pl.ds(base + 128, 128)]
            third = n_full[rows, pl.ds(base + 256, 128)]
            second_r = pltpu.roll(second, 64, 1)
            third_r = pltpu.roll(third, 64, 1)
            start = (p % 3) * 8 * 128 + (p // 3) * 64 + 2 * m
            n_left[pl.ds(start, 8, stride=128), :] = first
            n_right[pl.ds(start, 8, stride=128), :] = second
            n_left[pl.ds(start + 1, 8, stride=128), :] = jnp.where(low_half, second_r, third_r)
            n_right[pl.ds(start + 1, 8, stride=128), :] = third_r
        return _

    def split_n(i, _):
        rows = pl.ds(pl.multiple_of(i * 64, 64), 64)
        n_high[rows, 0:128], n_low[rows, 0:128] = split(n_left[rows])
        n_high[rows, 128:256], n_low[rows, 128:256] = split(n_right[rows])
        return _


    mbar = []
    for k in range(STAGES):
        mbar.append([
            pltpu.make_async_remote_copy(
                src_ref=mbar_out.at[2 * k + e],
                dst_ref=mbar_in.at[2 * k + e],
                send_sem=mbar_send.at[2 * k + e],
                recv_sem=mbar_recv.at[2 * k + e],
                device_id=(target(k, e), s),
                device_id_type=MESH,
            )
            for e in range(2)
        ])

    forward = [
        pltpu.make_async_remote_copy(
            src_ref=near[k],
            dst_ref=past[k],
            send_sem=fwd_send.at[k],
            recv_sem=fwd_recv.at[k],
            device_id=(sibling, s),
            device_id_type=MESH,
        )
        for k in range(STAGES)
    ]
    half_of = lax.broadcasted_iota(jnp.int32, (24, 128), 1) < 64

    def compute(k, e):
        pieces = []
        for q in range(3):
            name = q_list[0, 0, q]
            block = (past if e else near)[k][name // 2]
            piece = jnp.where(lax.rem(name, 2) == 0, block[:, :128], block[:, 128:])
            pieces.append(jnp.where(q < q_count[0, 0], piece, jnp.zeros_like(piece)))
        high, low = split(jnp.concatenate(pieces, axis=1))
        for j in range(6):
            cols = pl.ds(j * 256, 256)
            r = dot3(high, low, t_high[:, cols], t_low[:, cols])
            for i in range(2):
                r0 = r[:24, i * 128:(i + 1) * 128]
                r1 = r[24:, i * 128:(i + 1) * 128]
                even = jnp.where(half_of, r0, pltpu.roll(r1, 64, 1))
                odd = jnp.where(half_of, pltpu.roll(r0, 64, 1), r1)
                nu = j * 4 + i * 2
                for g in range(3):
                    mbar_out[2 * k + e, pl.ds(g * 192 + nu, 8, stride=24), :] = even[g * 8:(g + 1) * 8]
                    mbar_out[2 * k + e, pl.ds(g * 192 + nu + 1, 8, stride=24), :] = odd[g * 8:(g + 1) * 8]

    for copy in load_q:
        copy.wait()
    for k in range(STAGES):
        own[k].wait()
        for copy in chi[k]:
            copy.wait_recv()
        forward[k].start()
        if k < 3:
            for copy in chi[k + 1]:
                copy.start()
        compute(k, 0)
        if k < 3:
            mbar[k][0].start()
        forward[k].wait_recv()
        compute(k, 1)
        mbar[k][1].start()
        if k == 0:
            load_n.wait()
            lax.fori_loop(0, 32, lay_n, 0)
        if k == 1:
            lax.fori_loop(0, 48, split_n, 0)

    def side(o):
        return jnp.where(o < 3, -1, jnp.where(o > 4, 1, 0))

    def straddles(o):
        return jnp.logical_or(o == 2, o == 5)

    def part(i, o):
        return pltpu.make_async_remote_copy(
            src_ref=part_out.at[i], dst_ref=part_in.at[i], send_sem=part_send.at[i], recv_sem=part_recv.at[i],
            device_id=(o, atom(side(o))), device_id_type=MESH)

    def part_home(i, o):
        return pltpu.make_async_remote_copy(
            src_ref=part_out.at[i], dst_ref=home_in.at[i], send_sem=home_send.at[i], recv_sem=home_recv.at[i],
            device_id=(o, s), device_id_type=MESH)

    inner = side(t) == 0
    edge = straddles(t)

    for k in (3, 0, 1, 2):
        if k < 3:
            mbar[k][0].wait_recv()
        mbar[k][1].wait_recv()
        first = mbar_out if k == 3 else mbar_in
        acc = jnp.zeros((48, 256), F32)
        for g in range(6):
            highs, lows = [], []
            for p in range(4):
                rows = pl.ds((g * 4 + p) * 24, 24)
                high, low = split(jnp.concatenate([first[2 * k, rows, :], mbar_in[2 * k + 1, rows, :]], axis=0))
                highs.append(high)
                lows.append(low)
            rows = pl.ds(g * 512, 512)
            acc = acc + dot3(jnp.concatenate(highs, axis=1), jnp.concatenate(lows, axis=1), n_high[rows], n_low[rows])
        part_out[2 * k] = acc[:24]
        part_out[2 * k + 1] = acc[24:]
        for e in range(2):
            i, o = 2 * k + e, source(k, e)
            if i == 6:
                @pl.when(jnp.logical_not(inner))
                def _():
                    part(6, t).start()
            else:
                part(i, o).start()

                @pl.when(straddles(o))
                def _():
                    part_home(i, o).start()

    for k in range(STAGES):
        for copy in chi[k]:
            copy.wait_send()
        forward[k].wait_send()
        for e in range(2):
            if (k, e) != (3, 0):
                mbar[k][e].wait_send()

    order = (0, 1, 7, 2, 3, 4, 5)

    @pl.when(inner)
    def _():
        part_in[6] = part_out[6]

    @pl.when(jnp.logical_not(inner))
    def _():
        part(6, t).wait_recv()

    summed = part_in[6]
    for i in order:
        part(i, source(i // 2, i % 2)).wait_recv()
        summed = summed + part_in[i]
    total[...] = summed

    @pl.when(edge)
    def _():
        near_sum = part_out[6]
        for i in order:
            part_home(i, source(i // 2, i % 2)).wait_recv()
            near_sum = near_sum + home_in[i]
        row = lax.broadcasted_iota(jnp.int32, (24, 256), 0)
        least = jnp.where(t == 2, 16, 0)
        from_home = jnp.logical_and(row >= least, row < least + 8)
        total[...] = jnp.where(from_home, near_sum, total[...])

    def share(i):
        return pltpu.make_async_remote_copy(
            src_ref=total, dst_ref=final.at[t], send_sem=fin_send.at[i], recv_sem=fin_recv.at[n_tens - i],
            device_id=(lax.rem(t + i, n_tens), s), device_id_type=MESH)

    for i in (4, 3, 5, 2, 6, 1, 7):
        share(i).start()
    final[t] = total[...]
    for i in range(1, n_tens):
        share(i).wait_recv()

    lower = jnp.concatenate([final[5, 8:24, :], final[6], final[7]], axis=0)
    mid = jnp.concatenate([final[2, 16:24, :], final[3], final[4], final[5, 0:8, :]], axis=0)
    upper = jnp.concatenate([final[0], final[1], final[2, 0:16, :]], axis=0)
    half = lax.broadcasted_iota(jnp.int32, (64, 128), 1) < 64
    mid0 = pltpu.roll(mid[:, :128], 64, 1)
    mid1 = pltpu.roll(mid[:, 128:], 64, 1)
    zero = jnp.zeros((64, 128), F32)
    out[:, 0:128] = lower[:, :128] + jnp.where(half, zero, mid0)
    out[:, 128:256] = jnp.where(half, lower[:, 128:], zero) + jnp.where(half, mid0, mid1) + upper[:, :128]
    out[:, 256:320] = upper[:, 128:192]

    for i in order:
        o = source(i // 2, i % 2)
        part(i, o).wait_send()

        @pl.when(straddles(o))
        def _():
            part_home(i, o).wait_send()

    @pl.when(jnp.logical_not(inner))
    def _():
        part(6, t).wait_send()

    for i in range(1, n_tens):
        share(i).wait_send()


def local(n_tens, n_atom, chibar, t_blocks, n_saved, q_list, q_count):
    def body(*refs):
        kernel(n_tens, n_atom, *refs)

    hbm = pl.BlockSpec(memory_space=pltpu.HBM)
    dma = pltpu.SemaphoreType.DMA
    return pl.pallas_call(
        body,
        out_shape=jax.ShapeDtypeStruct((64, 320), F32),
        in_specs=[hbm] * 5,
        out_specs=pl.BlockSpec(memory_space=pltpu.VMEM),
        scratch_shapes=[
            pltpu.SMEM((1, 1, 3), jnp.int32),
            pltpu.SMEM((1, 1), jnp.int32),
            pltpu.VMEM((384, 1536), F32),
            pltpu.VMEM((384, 1536), BF16),
            pltpu.VMEM((384, 1536), BF16),
            pltpu.VMEM((48, 12288), F32),
            pltpu.VMEM((3072, 128), F32),
            pltpu.VMEM((3072, 128), F32),
            pltpu.VMEM((3072, 256), BF16),
            pltpu.VMEM((3072, 256), BF16),
        ]
        + [pltpu.VMEM((7, 48, 256), F32)] * (2 * STAGES)
        + [
            pltpu.VMEM((8, 576, 128), F32),
            pltpu.VMEM((8, 576, 128), F32),
            pltpu.VMEM((8, 24, 256), F32),
            pltpu.VMEM((8, 24, 256), F32),
            pltpu.VMEM((8, 24, 256), F32),
            pltpu.VMEM((24, 256), F32),
            pltpu.VMEM((8, 24, 256), F32),
            dma((2,)), dma, dma, dma((STAGES,)), dma((STAGES, 6)), dma((STAGES, 6)), dma((STAGES,)), dma((STAGES,)),
            dma((8,)), dma((8,)), dma((8,)), dma((8,)), dma((8,)), dma((8,)), dma((8,)), dma((8,)),
        ],
        compiler_params=pltpu.CompilerParams(
            collective_id=0, has_side_effects=True, vmem_limit_bytes=63 * 2**20
        ),
        name="gradient",
    )(chibar, t_blocks, n_saved, q_list, q_count)


def solution(mesh):
    sizes = mesh.shape
    placed = (
        P(None, "atom"),
        P(None, ("tens", "atom")),
        P("tens", "atom"),
        P("tens", "atom", None),
        P("tens", "atom"),
    )

    def step(*args):
        return local(sizes["tens"], sizes["atom"], *args)

    return jax.shard_map(step, mesh=mesh, in_specs=placed, out_specs=P("atom", None), check_vma=False)
```

```python
import jax
import jax.numpy as jnp
from jax import lax
from jax.experimental import pallas as pl
from jax.experimental.pallas import tpu as pltpu
from jax.sharding import PartitionSpec as P

F32 = jnp.float32
BF16 = jnp.bfloat16
MESH = pl.DeviceIdType.MESH
REACH = 3
STAGES = 4
SHIFTS = (1, -1, 2, -2, 3, -3)


def split(x):
    high = x.astype(BF16)
    return high, (x - high.astype(F32)).astype(BF16)


def dot(a, b):
    return jnp.dot(a, b, preferred_element_type=F32)


def dot3(a_high, a_low, b_high, b_low):
    rows = a_high.shape[0]
    both = dot(jnp.concatenate([a_high, a_low], axis=0), b_high)
    return both[:rows] + (both[rows:] + dot(a_high, b_low))


def kernel(n_tens, n_atom, chibar, t_blocks, n_saved, q_list_in, q_count_in, out, q_list, q_count,
           t_full, t_high, t_low, n_full, n_left, n_right, n_high, n_low,
           near0, near1, near2, near3, past0, past1, past2, past3, mbar_out, mbar_in, part_out, part_in, home_in, total, final,
           q_sem, t_sem, n_sem, own_sem, chi_send, chi_recv, fwd_send, fwd_recv,
           mbar_send, mbar_recv, part_send, part_recv, home_send, home_recv, fin_send, fin_recv):
    near = (near0, near1, near2, near3)
    past = (past0, past1, past2, past3)
    t = lax.axis_index("tens")
    s = lax.axis_index("atom")
    y = t // 2
    c = lax.rem(t, 2)
    chips = n_tens // 2

    def device(chip, core):
        return lax.rem(chip + chips, chips) * 2 + core

    def atom(by):
        return lax.rem(s + by + n_atom, n_atom)

    chip_to = (y + 2, y + 1 - 2 * c, y - 1 + 2 * c, y)
    chip_to2 = (y + 2, y - 1 + 2 * c, y + 1 - 2 * c, y)
    chip_from = (y + 2, y - 1 + 2 * c, y + 1 - 2 * c, y)

    def target(k, e):
        return device(chip_to[k], c) if e == 0 else device(chip_to2[k], 1 - c)

    def source(k, e):
        return device(chip_from[k], c if e == 0 else 1 - c)

    sibling = device(y, 1 - c)

    load_q = (pltpu.make_async_copy(q_list_in, q_list, q_sem.at[0]), pltpu.make_async_copy(q_count_in, q_count, q_sem.at[1]))
    for copy in load_q:
        copy.start()
    load_t = pltpu.make_async_copy(t_blocks, t_full, t_sem)
    load_n = pltpu.make_async_copy(n_saved, n_full, n_sem)
    own = []
    for k in range(STAGES):
        rows = pl.ds(pl.multiple_of(target(k, 0) * 48, 48), 48)
        own.append(pltpu.make_async_copy(chibar.at[rows], near[k].at[REACH], own_sem.at[k]))
        own[k].start()
    load_t.start()
    load_n.start()

    barrier = pltpu.get_barrier_semaphore()
    for by in SHIFTS:
        pl.semaphore_signal(barrier, inc=1, device_id=(t, atom(by)), device_id_type=MESH)
    for by in range(1, n_tens):
        pl.semaphore_signal(barrier, inc=1, device_id=(lax.rem(t + by, n_tens), s), device_id_type=MESH)
    pl.semaphore_wait(barrier, len(SHIFTS) + n_tens - 1)

    chi = []
    for k in range(STAGES):
        rows = pl.ds(pl.multiple_of(target(k, 0) * 48, 48), 48)
        chi.append([
            pltpu.make_async_remote_copy(
                src_ref=near[k].at[REACH],
                dst_ref=near[k].at[REACH - by],
                send_sem=chi_send.at[k, i],
                recv_sem=chi_recv.at[k, i],
                device_id=(t, atom(by)),
                device_id_type=MESH,
            )
            for i, by in enumerate(SHIFTS)
        ])
    for copy in own:
        copy.wait()
    for copy in chi[0]:
        copy.start()

    load_t.wait()

    def split_t(i, _):
        rows = pl.ds(pl.multiple_of(i * 16, 16), 16)
        t_high[rows], t_low[rows] = split(t_full[rows])
        return _

    lax.fori_loop(0, 24, split_t, 0)
    low_half = lax.broadcasted_iota(jnp.int32, (8, 128), 1) < 64

    def lay_n(m, _):
        base = pl.multiple_of(m * 384, 384)
        for p in range(6):
            rows = pl.ds(p * 8, 8)
            first = n_full[rows, pl.ds(base, 128)]
            second = n_full[rows, pl.ds(base + 128, 128)]
            third = n_full[rows, pl.ds(base + 256, 128)]
            second_r = pltpu.roll(second, 64, 1)
            third_r = pltpu.roll(third, 64, 1)
            start = (p % 3) * 8 * 128 + (p // 3) * 64 + 2 * m
            n_left[pl.ds(start, 8, stride=128), :] = first
            n_right[pl.ds(start, 8, stride=128), :] = second
            n_left[pl.ds(start + 1, 8, stride=128), :] = jnp.where(low_half, second_r, third_r)
            n_right[pl.ds(start + 1, 8, stride=128), :] = third_r
        return _

    def split_n(i, _):
        rows = pl.ds(pl.multiple_of(i * 64, 64), 64)
        n_high[rows, 0:128], n_low[rows, 0:128] = split(n_left[rows])
        n_high[rows, 128:256], n_low[rows, 128:256] = split(n_right[rows])
        return _


    mbar = []
    for k in range(STAGES):
        mbar.append([
            pltpu.make_async_remote_copy(
                src_ref=mbar_out.at[2 * k + e],
                dst_ref=mbar_in.at[2 * k + e],
                send_sem=mbar_send.at[2 * k + e],
                recv_sem=mbar_recv.at[2 * k + e],
                device_id=(target(k, e), s),
                device_id_type=MESH,
            )
            for e in range(2)
        ])

    forward = [
        pltpu.make_async_remote_copy(
            src_ref=near[k],
            dst_ref=past[k],
            send_sem=fwd_send.at[k],
            recv_sem=fwd_recv.at[k],
            device_id=(sibling, s),
            device_id_type=MESH,
        )
        for k in range(STAGES)
    ]
    half_of = lax.broadcasted_iota(jnp.int32, (24, 128), 1) < 64

    def compute(k, e):
        pieces = []
        for q in range(3):
            name = q_list[0, 0, q]
            block = (past if e else near)[k][name // 2]
            piece = jnp.where(lax.rem(name, 2) == 0, block[:, :128], block[:, 128:])
            pieces.append(jnp.where(q < q_count[0, 0], piece, jnp.zeros_like(piece)))
        high, low = split(jnp.concatenate(pieces, axis=1))
        for j in range(6):
            cols = pl.ds(j * 256, 256)
            r = dot3(high, low, t_high[:, cols], t_low[:, cols])
            for i in range(2):
                r0 = r[:24, i * 128:(i + 1) * 128]
                r1 = r[24:, i * 128:(i + 1) * 128]
                even = jnp.where(half_of, r0, pltpu.roll(r1, 64, 1))
                odd = jnp.where(half_of, pltpu.roll(r0, 64, 1), r1)
                nu = j * 4 + i * 2
                for g in range(3):
                    mbar_out[2 * k + e, pl.ds(g * 192 + nu, 8, stride=24), :] = even[g * 8:(g + 1) * 8]
                    mbar_out[2 * k + e, pl.ds(g * 192 + nu + 1, 8, stride=24), :] = odd[g * 8:(g + 1) * 8]

    for copy in load_q:
        copy.wait()
    for k in range(STAGES):
        for copy in chi[k]:
            copy.wait_recv()
        forward[k].start()
        if k < 3:
            for copy in chi[k + 1]:
                copy.start()
        compute(k, 0)
        if k < 3:
            mbar[k][0].start()
        forward[k].wait_recv()
        compute(k, 1)
        mbar[k][1].start()
        if k == 0:
            load_n.wait()
            lax.fori_loop(0, 32, lay_n, 0)
        if k == 1:
            lax.fori_loop(0, 48, split_n, 0)

    def side(o):
        return jnp.where(o < 3, -1, jnp.where(o > 4, 1, 0))

    def straddles(o):
        return jnp.logical_or(o == 2, o == 5)

    def part(i, o):
        return pltpu.make_async_remote_copy(
            src_ref=part_out.at[i], dst_ref=part_in.at[i], send_sem=part_send.at[i], recv_sem=part_recv.at[i],
            device_id=(o, atom(side(o))), device_id_type=MESH)

    def part_home(i, o):
        return pltpu.make_async_remote_copy(
            src_ref=part_out.at[i], dst_ref=home_in.at[i], send_sem=home_send.at[i], recv_sem=home_recv.at[i],
            device_id=(o, s), device_id_type=MESH)

    inner = side(t) == 0
    edge = straddles(t)

    for k in (3, 0, 1, 2):
        if k < 3:
            mbar[k][0].wait_recv()
        mbar[k][1].wait_recv()
        first = mbar_out if k == 3 else mbar_in
        acc = jnp.zeros((48, 256), F32)
        for g in range(6):
            highs, lows = [], []
            for p in range(4):
                rows = pl.ds((g * 4 + p) * 24, 24)
                high, low = split(jnp.concatenate([first[2 * k, rows, :], mbar_in[2 * k + 1, rows, :]], axis=0))
                highs.append(high)
                lows.append(low)
            rows = pl.ds(g * 512, 512)
            acc = acc + dot3(jnp.concatenate(highs, axis=1), jnp.concatenate(lows, axis=1), n_high[rows], n_low[rows])
        part_out[2 * k] = acc[:24]
        part_out[2 * k + 1] = acc[24:]
        for e in range(2):
            i, o = 2 * k + e, source(k, e)
            if i == 6:
                @pl.when(jnp.logical_not(inner))
                def _():
                    part(6, t).start()
            else:
                part(i, o).start()

                @pl.when(straddles(o))
                def _():
                    part_home(i, o).start()

    for k in range(STAGES):
        for copy in chi[k]:
            copy.wait_send()
        forward[k].wait_send()
        for e in range(2):
            if (k, e) != (3, 0):
                mbar[k][e].wait_send()

    order = (0, 1, 7, 2, 3, 4, 5)

    @pl.when(inner)
    def _():
        part_in[6] = part_out[6]

    @pl.when(jnp.logical_not(inner))
    def _():
        part(6, t).wait_recv()

    summed = part_in[6]
    for i in order:
        part(i, source(i // 2, i % 2)).wait_recv()
        summed = summed + part_in[i]
    total[...] = summed

    @pl.when(edge)
    def _():
        near_sum = part_out[6]
        for i in order:
            part_home(i, source(i // 2, i % 2)).wait_recv()
            near_sum = near_sum + home_in[i]
        row = lax.broadcasted_iota(jnp.int32, (24, 256), 0)
        least = jnp.where(t == 2, 16, 0)
        from_home = jnp.logical_and(row >= least, row < least + 8)
        total[...] = jnp.where(from_home, near_sum, total[...])

    def share(i):
        return pltpu.make_async_remote_copy(
            src_ref=total, dst_ref=final.at[t], send_sem=fin_send.at[i], recv_sem=fin_recv.at[n_tens - i],
            device_id=(lax.rem(t + i, n_tens), s), device_id_type=MESH)

    for i in (4, 3, 5, 2, 6, 1, 7):
        share(i).start()
    final[t] = total[...]
    for i in order:
        o = source(i // 2, i % 2)
        part(i, o).wait_send()

        @pl.when(straddles(o))
        def _():
            part_home(i, o).wait_send()

    @pl.when(jnp.logical_not(inner))
    def _():
        part(6, t).wait_send()

    for i in range(1, n_tens):
        share(i).wait_recv()

    lower = jnp.concatenate([final[5, 8:24, :], final[6], final[7]], axis=0)
    mid = jnp.concatenate([final[2, 16:24, :], final[3], final[4], final[5, 0:8, :]], axis=0)
    upper = jnp.concatenate([final[0], final[1], final[2, 0:16, :]], axis=0)
    half = lax.broadcasted_iota(jnp.int32, (64, 128), 1) < 64
    mid0 = pltpu.roll(mid[:, :128], 64, 1)
    mid1 = pltpu.roll(mid[:, 128:], 64, 1)
    zero = jnp.zeros((64, 128), F32)
    out[:, 0:128] = lower[:, :128] + jnp.where(half, zero, mid0)
    out[:, 128:256] = jnp.where(half, lower[:, 128:], zero) + jnp.where(half, mid0, mid1) + upper[:, :128]
    out[:, 256:320] = upper[:, 128:192]

    for i in range(1, n_tens):
        share(i).wait_send()


def local(n_tens, n_atom, chibar, t_blocks, n_saved, q_list, q_count):
    def body(*refs):
        kernel(n_tens, n_atom, *refs)

    hbm = pl.BlockSpec(memory_space=pltpu.HBM)
    dma = pltpu.SemaphoreType.DMA
    return pl.pallas_call(
        body,
        out_shape=jax.ShapeDtypeStruct((64, 320), F32),
        in_specs=[hbm] * 5,
        out_specs=pl.BlockSpec(memory_space=pltpu.VMEM),
        scratch_shapes=[
            pltpu.SMEM((1, 1, 3), jnp.int32),
            pltpu.SMEM((1, 1), jnp.int32),
            pltpu.VMEM((384, 1536), F32),
            pltpu.VMEM((384, 1536), BF16),
            pltpu.VMEM((384, 1536), BF16),
            pltpu.VMEM((48, 12288), F32),
            pltpu.VMEM((3072, 128), F32),
            pltpu.VMEM((3072, 128), F32),
            pltpu.VMEM((3072, 256), BF16),
            pltpu.VMEM((3072, 256), BF16),
        ]
        + [pltpu.VMEM((7, 48, 256), F32)] * (2 * STAGES)
        + [
            pltpu.VMEM((8, 576, 128), F32),
            pltpu.VMEM((8, 576, 128), F32),
            pltpu.VMEM((8, 24, 256), F32),
            pltpu.VMEM((8, 24, 256), F32),
            pltpu.VMEM((8, 24, 256), F32),
            pltpu.VMEM((24, 256), F32),
            pltpu.VMEM((8, 24, 256), F32),
            dma((2,)), dma, dma, dma((STAGES,)), dma((STAGES, 6)), dma((STAGES, 6)), dma((STAGES,)), dma((STAGES,)),
            dma((8,)), dma((8,)), dma((8,)), dma((8,)), dma((8,)), dma((8,)), dma((8,)), dma((8,)),
        ],
        compiler_params=pltpu.CompilerParams(
            collective_id=0, has_side_effects=True, vmem_limit_bytes=63 * 2**20
        ),
        name="gradient",
    )(chibar, t_blocks, n_saved, q_list, q_count)


def solution(mesh):
    sizes = mesh.shape
    placed = (
        P(None, "atom"),
        P(None, ("tens", "atom")),
        P("tens", "atom"),
        P("tens", "atom", None),
        P("tens", "atom"),
    )

    def step(*args):
        return local(sizes["tens"], sizes["atom"], *args)

    return jax.shard_map(step, mesh=mesh, in_specs=placed, out_specs=P("atom", None), check_vma=False)
```
